32 devices in a mesh: layer: 2 (over x), row: 16 (over z, y, core).
Axes of the slice: x: 2, y: 2, z: 4, core: 2. Of those that a mesh axis runs over, the one named last changes fastest.
Arguments:
- deltas: bfloat16 [2, 2, 1024, 16384], P('layer', None, 'row'), parts along dimension 0, may hold values from -6 to 6
- basis: bfloat16 [16384, 128], P('row'), may hold values from -0.046875 to 0.046875
Outputs:
- merged: bfloat16 [2, 1024, 16384], P('layer', None, 'row'), parts along dimension 0
The draws below stay inside these ranges and needn't reach their ends.
There are 2 independent parts, one for each index of `layer`. The reference program is written for one: setup_inputs(seed, part) draws one part's arguments, and reference() takes and returns one part's arrays. A program takes and returns all parts, laid end to end along the dimension named above; an argument that names none is the same for every part. Nothing has to cross between parts.
All inputs are finite; a program needn't handle non-finite values.
Results may differ from the reference program's by a relative error of at most 0.0081.
Values may be sent and summed in bfloat16 or wider, within the bound.
A program may use at most 64 MiB of HBM per device.

```python
import jax
import jax.numpy as jnp
from jax import lax

GROUP = 1
TASKS = 2
RANK = 128
COLS = 16384
ROWS = 1024


def levels(key, dims, cuts, low, top_value):
    def one(axis_at, shards_of):
        heights = jax.random.uniform(jax.random.fold_in(jax.random.fold_in(key, 6), axis_at), (shards_of,), jnp.float32, low / len(cuts), top_value / len(cuts))
        return jnp.repeat(jnp.exp(heights), dims[axis_at] // shards_of).reshape((-1,) + (1,) * (len(dims) - axis_at - 1))

    gain = one(*cuts[0])
    for cut in cuts[1:]:
        gain = gain * one(*cut)
    return gain


def gaussian(own_key, extent, scale, reach, shards=(), kind=jnp.bfloat16):
    loudness = levels(own_key, extent, shards, -0.22, 0.18) if shards else 1.0
    result = jax.random.normal(own_key, extent, jnp.float32) * scale * loudness
    return jnp.minimum(jnp.maximum(result, -reach), reach).astype(kind)


def setup_inputs(seed: int = 0, part: int = 0) -> dict:
    keys = jax.random.split(jax.random.key(seed), 3)
    part_keys = jax.random.split(jax.random.fold_in(keys[2], part), 3)
    return {
        "deltas": gaussian(part_keys[0], (GROUP, TASKS, ROWS, COLS), 1.0, 6.0, ((2, 16),)),
        "basis": gaussian(keys[1], (COLS, RANK), COLS ** -0.5, 0.046875, ((0, 16),)),
    }


def reference(deltas, basis):
    group_deltas = deltas[0]
    sketches = []
    for task in range(TASKS):
        sketches.append(jnp.dot(group_deltas[task].astype(jnp.float32), basis.astype(jnp.float32), preferred_element_type=jnp.float32).astype(jnp.bfloat16))
    factors = jnp.concatenate(sketches, axis=1)
    gram_sum = jnp.dot(factors.T.astype(jnp.float32), factors.astype(jnp.float32), preferred_element_type=jnp.float32)
    chol_factor = jnp.linalg.cholesky(gram_sum)
    whitened = lax.linalg.triangular_solve(chol_factor, factors.astype(gram_sum.dtype), left_side=False, lower=True, transpose_a=True).astype(jnp.bfloat16)
    summed = group_deltas[0].astype(gram_sum.dtype)
    for task in range(1, TASKS):
        summed = summed + group_deltas[task].astype(gram_sum.dtype)
    task_sum = summed.astype(jnp.bfloat16)
    coeffs = jnp.dot(whitened.T.astype(jnp.float32), task_sum.astype(jnp.float32), preferred_element_type=jnp.float32).astype(jnp.bfloat16)
    merged = jnp.dot(whitened.astype(jnp.float32), coeffs.astype(jnp.float32), preferred_element_type=jnp.float32).astype(jnp.bfloat16)
    return merged[None]
```

```python
import functools

import jax
import jax.numpy as jnp
from jax import lax
from jax.experimental import pallas as pl
from jax.experimental.pallas import tpu as pltpu
from jax.sharding import PartitionSpec as P

MESH = pl.DeviceIdType.MESH
F32 = jnp.float32
BF16 = jnp.bfloat16
EXACT = lax.Precision.HIGHEST
PANEL = 32
GROUP = 8


def whiten_rows(factors, chol_factor):
    return lax.linalg.triangular_solve(
        chol_factor, factors.astype(jnp.float32), left_side=False, lower=True, transpose_a=True
    ).astype(jnp.bfloat16)


def inner_rows(left, right):
    return lax.dot_general(
        left, right, (((0,), (0,)), ((), ())), preferred_element_type=jnp.float32
    )


def outer_rows(left, right):
    return lax.dot_general(
        left, right, (((1,), (1,)), ((), ())), preferred_element_type=jnp.float32
    )


def general_shards(deltas, basis):
    group_deltas = deltas[0]
    task_count, rows_local, col_count = group_deltas.shape
    rank_width = basis.shape[1]
    factor_width = task_count * rank_width
    sketch = jnp.einsum(
        "trc,ck->trk",
        group_deltas,
        lax.all_gather(basis, "row", axis=0, tiled=True),
        preferred_element_type=jnp.float32,
    )
    factors = sketch.astype(jnp.bfloat16).transpose(1, 0, 2).reshape(rows_local, factor_width)
    gram_sum = lax.psum(inner_rows(factors, factors), "row")
    chol_factor = jnp.linalg.cholesky(gram_sum)
    local_white = whiten_rows(factors, chol_factor)
    whitened = lax.all_gather(local_white, "row", axis=0, tiled=True)
    task_sum = jnp.sum(group_deltas.astype(jnp.float32), axis=0).astype(jnp.bfloat16)
    columns = lax.all_to_all(task_sum, "row", split_axis=1, concat_axis=0, tiled=True)
    coeffs = inner_rows(columns, whitened).astype(jnp.bfloat16)
    merged = lax.dot_general(
        whitened, coeffs, (((1,), (1,)), ((), ())), preferred_element_type=jnp.float32
    )
    return merged.astype(jnp.bfloat16)[None]


def panel_inverse(block):
    shape = block.shape
    row = lax.broadcasted_iota(jnp.int32, shape, 0)
    lane = lax.broadcasted_iota(jnp.int32, shape, 1)
    work = jnp.where(lane < PANEL, block, 0.0) + jnp.where(lane == row + PANEL, 1.0, 0.0)
    pivots = jnp.ones(shape, F32)
    for start in range(0, PANEL, GROUP):
        cols = [
            jnp.broadcast_to(work[:, j : j + 1], shape) for j in range(start, start + GROUP)
        ]
        for at in range(GROUP):
            j = start + at
            pivot = cols[at][j : j + 1, :]
            pivots = jnp.where(row == j, pivot, pivots)
            scale = jnp.where(row > j, cols[at] * (1.0 / pivot), 0.0)
            work = work - scale * work[j : j + 1, :]
            for later in range(at + 1, GROUP):
                cols[later] = cols[later] - scale * cols[later][j : j + 1, :]
    root = lax.rsqrt(pivots)
    root = root * (1.5 - 0.5 * pivots * root * root)
    return (work * root)[:, PANEL : 2 * PANEL]


def chol_inverse(aug):
    size = aug.shape[0]

    @pl.loop(0, size // PANEL)
    def _(k):
        at = pl.multiple_of(k * PANEL, PANEL)
        rows = aug[pl.ds(at, PANEL), :]
        turned = pltpu.roll(rows[:, :size], lax.rem(size - at, size), 1)
        inverse = panel_inverse(turned[:, :128])
        done = lax.dot_general(
            inverse, rows, (((1,), (0,)), ((), ())), precision=EXACT, preferred_element_type=F32
        )
        lane = lax.broadcasted_iota(jnp.int32, (PANEL, size), 1)
        below = jnp.where(lane >= at + PANEL, done[:, :size], 0.0)
        aug[...] -= lax.dot_general(
            below, done, (((0,), (0,)), ((), ())), precision=EXACT, preferred_element_type=F32
        )
        aug[pl.ds(at, PANEL), :] = done


def kernel(
    lines,
    deltas,
    basis,
    white,
    coeffs,
    held,
    sums,
    columns,
    bases,
    factors,
    sketch,
    aug,
    total,
    load_sem,
    basis_line,
    basis_side,
    basis_over,
    basis_core,
    basis_recv,
    sum_send,
    sum_recv,
    factor_line,
    factor_side,
    factor_core,
    factor_recv,
):
    layer = lax.axis_index("layer")
    me = lax.axis_index("row")
    z, y, c = me // 4, lax.rem(me // 2, 2), lax.rem(me, 2)
    n = 4 * lines
    depth = basis.shape[0]
    half = depth // 2
    tasks, rows_local, _ = held.shape
    width = columns.shape[1]

    def row_of(zz, yy, cc):
        return (zz * 2 + yy) * 2 + cc

    chunk = held.shape[2] // 4
    loads = []
    for i in range(4):
        load = pltpu.make_async_copy(
            deltas.at[:, :, pl.ds(i * chunk, chunk)],
            held.at[:, :, pl.ds(i * chunk, chunk)],
            load_sem.at[i],
        )
        load.start()
        loads.append(load)

    barrier = pltpu.get_barrier_semaphore()
    for k in range(1, n):
        pl.semaphore_signal(
            barrier, inc=1, device_id=(layer, lax.rem(me + k, n)), device_id_type=MESH
        )
    pl.semaphore_signal(barrier, inc=1, device_id=(1 - layer, me), device_id_type=MESH)
    bases[me] = basis[...]
    sketch[...] = jnp.zeros_like(sketch)
    pl.semaphore_wait(barrier, n)

    sent = []

    def start(copy, valid=None):
        if valid is None:
            copy.start()
        else:
            pl.when(valid)(copy.start)
        sent.append((copy, valid))

    def basis_copy(block, part, sem, to):
        place = bases.at[block, pl.ds(pl.multiple_of(part * half, half), half), :]
        return pltpu.make_async_remote_copy(
            src_ref=place,
            dst_ref=place,
            send_sem=sem,
            recv_sem=basis_recv.at[block, part],
            device_id=to,
            device_id_type=MESH,
        )

    def got_basis(block, part):
        basis_copy(block, part, basis_core.at[block, part], (1 - layer, me)).wait_recv()

    def to_side(block, valid=None):
        start(
            basis_copy(block, layer, basis_side.at[block], (layer, row_of(z, 1 - y, c))), valid
        )

    def to_over(block, valid=None):
        start(basis_copy(block, layer, basis_over.at[block], (1 - layer, me)), valid)

    def to_core(block, part, valid=None):
        start(
            basis_copy(
                block, part, basis_core.at[block, part], (layer, row_of(z, y, 1 - c))
            ),
            valid,
        )

    def to_line(block, step, valid):
        start(
            basis_copy(block, layer, basis_line.at[block, (step + 1) // 2], (layer, row_of(z + step, y, c))),
            valid,
        )

    def use_basis(block):
        at = pl.multiple_of(block * depth, depth)
        for t in range(tasks):
            sketch[t] += jnp.dot(
                held[t, :, pl.ds(at, depth)], bases[block], preferred_element_type=F32
            )

    def when(valid, run):
        if valid is None:
            run()
        else:
            pl.when(valid)(run)

    def at_distance(d):
        if d == 0:
            return [(z, 0, None)]
        return [(z - d, -1, z - d >= 0), (z + d, 1, z + d < lines)]

    to_line(me, 1, z + 1 < lines)
    to_line(me, -1, z >= 1)
    to_side(me)
    to_core(me, layer)
    to_core(me, 1 - layer)

    for load in loads:
        load.wait()

    def sum_copy(k):
        to = lax.rem(me + k, n)
        return pltpu.make_async_remote_copy(
            src_ref=sums.at[to],
            dst_ref=columns.at[pl.ds(pl.multiple_of(me * rows_local, rows_local), rows_local), :],
            send_sem=sum_send.at[to],
            recv_sem=sum_recv.at[me],
            device_id=(layer, to),
            device_id_type=MESH,
        )

    def got_sum(source):
        pltpu.make_async_remote_copy(
            src_ref=sums.at[source],
            dst_ref=columns.at[
                pl.ds(pl.multiple_of(source * rows_local, rows_local), rows_local), :
            ],
            send_sem=sum_send.at[source],
            recv_sem=sum_recv.at[source],
            device_id=(1 - layer, me),
            device_id_type=MESH,
        ).wait_recv()

    def task_sum(to):
        at = pl.ds(pl.multiple_of(to * width, width), width)
        result = held[0, :, at].astype(F32)
        for t in range(1, tasks):
            result = result + held[t, :, at].astype(F32)
        return result.astype(BF16)

    @pl.loop(1, n)
    def _(k):
        to = lax.rem(me + k, n)
        sums[to] = task_sum(to)
        sum_copy(k).start()

    columns[pl.ds(pl.multiple_of(me * rows_local, rows_local), rows_local), :] = task_sum(me)
    use_basis(me)

    for tick in range(lines + 3):
        if 1 <= tick < lines:
            for zz, step, valid in at_distance(tick):
                block = row_of(zz, y, c)
                when(valid, functools.partial(got_basis, block, layer))
                onward = z + 1 < lines if step < 0 else z >= 1
                to_line(block, -step, jnp.logical_and(valid, onward))
                to_side(block, valid)
                to_over(block, valid)
                to_core(block, layer, valid)
        if 0 <= tick - 1 < lines:
            for zz, _, valid in at_distance(tick - 1):
                block = row_of(zz, 1 - y, c)
                when(valid, functools.partial(got_basis, block, layer))
                to_over(block, valid)
                to_core(block, layer, valid)
        if 0 <= tick - 2 < lines:
            for zz, _, valid in at_distance(tick - 2):
                for yy in (y, 1 - y):
                    if tick == 2 and yy is y:
                        continue
                    block = row_of(zz, yy, c)
                    when(valid, functools.partial(got_basis, block, 1 - layer))
                    to_core(block, 1 - layer, valid)
                    when(valid, functools.partial(use_basis, block))
        if 0 <= tick - 3 < lines:
            for zz, _, valid in at_distance(tick - 3):
                for yy in (y, 1 - y):
                    block = row_of(zz, yy, 1 - c)
                    when(valid, functools.partial(got_basis, block, layer))
                    when(valid, functools.partial(got_basis, block, 1 - layer))
                    when(valid, functools.partial(use_basis, block))

    def factor_place(block):
        return factors.at[pl.ds(pl.multiple_of(block * rows_local, rows_local), rows_local), :]

    def factor_copy(block, sem, to):
        return pltpu.make_async_remote_copy(
            src_ref=factor_place(block),
            dst_ref=factor_place(block),
            send_sem=sem,
            recv_sem=factor_recv.at[block],
            device_id=(layer, to),
            device_id_type=MESH,
        )

    def got_factor(block):
        factor_copy(block, factor_core.at[block], row_of(z, y, 1 - c)).wait_recv()

    own = [sketch[t].astype(BF16) for t in range(tasks)]
    factors[pl.ds(pl.multiple_of(me * rows_local, rows_local), rows_local), :] = jnp.concatenate(
        own, axis=1
    )
    for k in range(1, lines):
        to = row_of(lax.rem(z + k, lines), y, c)
        start(factor_copy(me, factor_line.at[k], to))

    def factor_to_side(block):
        start(factor_copy(block, factor_side.at[block], row_of(z, 1 - y, c)))

    def factor_to_core(block):
        start(factor_copy(block, factor_core.at[block], row_of(z, y, 1 - c)))

    factor_to_side(me)
    factor_to_core(me)
    for k in range(1, lines):
        block = row_of(lax.rem(z + k, lines), y, c)
        got_factor(block)
        factor_to_side(block)
        factor_to_core(block)
    for k in range(lines):
        block = row_of(lax.rem(z + k, lines), 1 - y, c)
        got_factor(block)
        factor_to_core(block)
    for k in range(lines):
        for yy in (y, 1 - y):
            got_factor(row_of(lax.rem(z + k, lines), yy, 1 - c))

    size = aug.shape[0]
    aug[:, :size] = inner_rows(factors[...], factors[...])
    aug[:, size:] = jnp.where(
        lax.broadcasted_iota(jnp.int32, (size, size), 0)
        == lax.broadcasted_iota(jnp.int32, (size, size), 1),
        1.0,
        0.0,
    )
    chol_inverse(aug)
    rest = aug[:, size:]
    result = None
    for _ in range(3):
        piece = rest.astype(BF16)
        rest = rest - piece.astype(F32)
        term = outer_rows(factors[...], piece)
        result = term if result is None else result + term
    white[...] = result.astype(BF16)

    group = 4 * rows_local
    for k in range(lines):
        zz = lax.rem(z + k, lines)
        for yy, cc in ((y, c), (y, 1 - c), (1 - y, c), (1 - y, 1 - c)):
            if k == 0 and yy is y and cc is c:
                continue
            got_sum(row_of(zz, yy, cc))
        at = pl.ds(pl.multiple_of(zz * group, group), group)
        term = inner_rows(white[at, :], columns[at, :])
        if k == 0:
            total[...] = term
        elif k < lines - 1:
            total[...] += term
        else:
            coeffs[...] = (total[...] + term).astype(BF16)

    for copy, valid in sent:
        when(valid, copy.wait_send)

    @pl.loop(1, n)
    def _(k):
        sum_copy(k).wait_send()


def line_shards(n, deltas, basis):
    tasks, rows_local, cols = deltas.shape[1:]
    depth, rank = basis.shape
    size = tasks * rank
    width = cols // n
    rows = rows_local * n
    lines = n // 4
    dma = pltpu.SemaphoreType.DMA
    white, coeffs = pl.pallas_call(
        functools.partial(kernel, lines),
        out_shape=(
            jax.ShapeDtypeStruct((rows, size), BF16),
            jax.ShapeDtypeStruct((size, width), BF16),
        ),
        in_specs=[
            pl.BlockSpec(memory_space=pl.ANY),
            pl.BlockSpec(memory_space=pltpu.VMEM),
        ],
        out_specs=[pl.BlockSpec(memory_space=pltpu.VMEM)] * 2,
        scratch_shapes=[
            pltpu.VMEM((tasks, rows_local, cols), BF16),
            pltpu.VMEM((n, rows_local, width), BF16),
            pltpu.VMEM((rows, width), BF16),
            pltpu.VMEM((n, depth, rank), BF16),
            pltpu.VMEM((rows, size), BF16),
            pltpu.VMEM((tasks, rows_local, rank), F32),
            pltpu.VMEM((size, 2 * size), F32),
            pltpu.VMEM((size, width), F32),
            dma((4,)),
            dma((n, 2)),
            dma((n,)),
            dma((n,)),
            dma((n, 2)),
            dma((n, 2)),
            dma((n,)),
            dma((n,)),
            dma((lines,)),
            dma((n,)),
            dma((n,)),
            dma((n,)),
        ],
        compiler_params=pltpu.CompilerParams(
            collective_id=0, has_side_effects=True, vmem_limit_bytes=48 * 2**20
        ),
        cost_estimate=pl.CostEstimate(
            flops=4 * rows * size * width, bytes_accessed=8 * 2**20, transcendentals=0
        ),
    )(deltas[0], basis)
    merged = lax.dot_general(
        white, coeffs, (((1,), (0,)), ((), ())), preferred_element_type=F32
    )
    return merged.astype(BF16)[None]


def solution(mesh):
    n = mesh.shape["row"]
    fits = n == 16 and mesh.shape["layer"] == 2
    return jax.shard_map(
        functools.partial(line_shards, n) if fits else general_shards,
        mesh=mesh,
        in_specs=(P("layer", None, "row", None), P("row", None)),
        out_specs=P("layer", None, "row"),
        check_vma=False,
    )
```

```python
import functools

import jax
import jax.numpy as jnp
from jax import lax
from jax.experimental import pallas as pl
from jax.experimental.pallas import tpu as pltpu
from jax.sharding import PartitionSpec as P

MESH = pl.DeviceIdType.MESH
F32 = jnp.float32
BF16 = jnp.bfloat16
EXACT = lax.Precision.HIGHEST
PANEL = 64
GROUP = 16
PACE = (0, 1, 1, 1, 1, 1, 1, 0)


def whiten_rows(factors, chol_factor):
    return lax.linalg.triangular_solve(
        chol_factor, factors.astype(jnp.float32), left_side=False, lower=True, transpose_a=True
    ).astype(jnp.bfloat16)


def inner_rows(left, right):
    return lax.dot_general(
        left, right, (((0,), (0,)), ((), ())), preferred_element_type=jnp.float32
    )


def outer_rows(left, right):
    return lax.dot_general(
        left, right, (((1,), (1,)), ((), ())), preferred_element_type=jnp.float32
    )


def general_shards(deltas, basis):
    group_deltas = deltas[0]
    task_count, rows_local, col_count = group_deltas.shape
    rank_width = basis.shape[1]
    factor_width = task_count * rank_width
    sketch = jnp.einsum(
        "trc,ck->trk",
        group_deltas,
        lax.all_gather(basis, "row", axis=0, tiled=True),
        preferred_element_type=jnp.float32,
    )
    factors = sketch.astype(jnp.bfloat16).transpose(1, 0, 2).reshape(rows_local, factor_width)
    gram_sum = lax.psum(inner_rows(factors, factors), "row")
    chol_factor = jnp.linalg.cholesky(gram_sum)
    local_white = whiten_rows(factors, chol_factor)
    whitened = lax.all_gather(local_white, "row", axis=0, tiled=True)
    task_sum = jnp.sum(group_deltas.astype(jnp.float32), axis=0).astype(jnp.bfloat16)
    columns = lax.all_to_all(task_sum, "row", split_axis=1, concat_axis=0, tiled=True)
    coeffs = inner_rows(columns, whitened).astype(jnp.bfloat16)
    merged = lax.dot_general(
        whitened, coeffs, (((1,), (1,)), ((), ())), preferred_element_type=jnp.float32
    )
    return merged.astype(jnp.bfloat16)[None]


def panel_inverse(block):
    shape = block.shape
    row = lax.broadcasted_iota(jnp.int32, shape, 0)
    lane = lax.broadcasted_iota(jnp.int32, shape, 1)
    work = jnp.where(lane < PANEL, block, 0.0) + jnp.where(lane == row + PANEL, 1.0, 0.0)
    pivots = jnp.ones(shape, F32)
    for start in range(0, PANEL, GROUP):
        cols = [
            jnp.broadcast_to(work[:, j : j + 1], shape) for j in range(start, start + GROUP)
        ]
        for at in range(GROUP):
            j = start + at
            pivot = cols[at][j : j + 1, :]
            pivots = jnp.where(row == j, pivot, pivots)
            scale = jnp.where(row > j, cols[at] * (1.0 / pivot), 0.0)
            work = work - scale * work[j : j + 1, :]
            for later in range(at + 1, GROUP):
                cols[later] = cols[later] - scale * cols[later][j : j + 1, :]
    root = lax.rsqrt(pivots)
    root = root * (1.5 - 0.5 * pivots * root * root)
    return (work * root)[:, PANEL : 2 * PANEL]


def chol_inverse(aug):
    size = aug.shape[0]
    for at in range(0, size, PANEL):
        after = at + PANEL
        rows = aug[at:after, :]
        inverse = panel_inverse(rows[:, at : at + 128] if at % 128 == 0 else pltpu.roll(
            rows[:, at - at % 128 : at - at % 128 + 128], 128 - at % 128, 1
        ))
        done = lax.dot_general(
            inverse, rows, (((1,), (0,)), ((), ())), precision=EXACT, preferred_element_type=F32
        )
        if after < size:
            aug[after:, :] -= lax.dot_general(
                done[:, after:size],
                done,
                (((0,), (0,)), ((), ())),
                precision=EXACT,
                preferred_element_type=F32,
            )
        aug[at:after, :] = done


def kernel(
    lines,
    deltas,
    basis,
    white,
    coeffs,
    held,
    sums,
    columns,
    bases,
    factors,
    sketch,
    aug,
    total,
    load_sem,
    basis_line,
    basis_side,
    basis_over,
    basis_core,
    basis_recv,
    sum_send,
    sum_recv,
    factor_line,
    factor_side,
    factor_core,
    factor_recv,
):
    layer = lax.axis_index("layer")
    me = lax.axis_index("row")
    z, y, c = me // 4, lax.rem(me // 2, 2), lax.rem(me, 2)
    n = 4 * lines
    depth = basis.shape[0]
    half = depth // 2
    tasks, rows_local, _ = held.shape
    width = columns.shape[1]

    def row_of(zz, yy, cc):
        return (zz * 2 + yy) * 2 + cc

    chunk = held.shape[2] // 4
    loads = []
    for i in range(4):
        load = pltpu.make_async_copy(
            deltas.at[:, :, pl.ds(i * chunk, chunk)],
            held.at[:, :, pl.ds(i * chunk, chunk)],
            load_sem.at[i],
        )
        load.start()
        loads.append(load)

    own_basis = pltpu.make_async_copy(basis, bases.at[me], load_sem.at[4])
    own_basis.start()

    barrier = pltpu.get_barrier_semaphore()
    for k in range(1, n):
        pl.semaphore_signal(
            barrier, inc=1, device_id=(layer, lax.rem(me + k, n)), device_id_type=MESH
        )
    pl.semaphore_signal(barrier, inc=1, device_id=(1 - layer, me), device_id_type=MESH)
    sketch[...] = jnp.zeros_like(sketch)
    own_basis.wait()
    pl.semaphore_wait(barrier, n)

    sent = []

    def start(copy, valid=None):
        if valid is None:
            copy.start()
        else:
            pl.when(valid)(copy.start)
        sent.append((copy, valid))

    def basis_copy(block, part, sem, to):
        place = bases.at[block, pl.ds(pl.multiple_of(part * half, half), half), :]
        return pltpu.make_async_remote_copy(
            src_ref=place,
            dst_ref=place,
            send_sem=sem,
            recv_sem=basis_recv.at[block, part],
            device_id=to,
            device_id_type=MESH,
        )

    def got_basis(block, part):
        basis_copy(block, part, basis_core.at[block, part], (1 - layer, me)).wait_recv()

    def to_side(block, part, valid=None):
        start(
            basis_copy(
                block, part, basis_side.at[block, part], (layer, row_of(z, 1 - y, c))
            ),
            valid,
        )

    def to_over(block, valid=None):
        start(basis_copy(block, layer, basis_over.at[block], (1 - layer, me)), valid)

    def to_core(block, part, valid=None):
        start(
            basis_copy(
                block, part, basis_core.at[block, part], (layer, row_of(z, y, 1 - c))
            ),
            valid,
        )

    def to_line(block, step, valid):
        start(
            basis_copy(block, layer, basis_line.at[block, (step + 1) // 2], (layer, row_of(z + step, y, c))),
            valid,
        )

    def use_basis(block):
        at = pl.multiple_of(block * depth, depth)
        left = held[:, :, pl.ds(at, depth)].reshape(tasks * rows_local, depth)
        sketch[...] += jnp.dot(left, bases[block], preferred_element_type=F32).reshape(sketch.shape)

    def when(valid, run):
        if valid is None:
            run()
        else:
            pl.when(valid)(run)

    def at_distance(d):
        if d == 0:
            return [(z, 0, None)]
        return [(z - d, -1, z - d >= 0), (z + d, 1, z + d < lines)]

    to_line(me, 1, z + 1 < lines)
    to_line(me, -1, z >= 1)
    to_side(me, layer)
    to_side(me, 1 - layer)
    to_core(me, layer)
    to_core(me, 1 - layer)

    def sum_copy(to):
        return pltpu.make_async_remote_copy(
            src_ref=sums.at[to],
            dst_ref=columns.at[pl.ds(pl.multiple_of(me * rows_local, rows_local), rows_local), :],
            send_sem=sum_send.at[to],
            recv_sem=sum_recv.at[me],
            device_id=(layer, to),
            device_id_type=MESH,
        )

    def got_sum(source):
        pltpu.make_async_remote_copy(
            src_ref=sums.at[source],
            dst_ref=columns.at[
                pl.ds(pl.multiple_of(source * rows_local, rows_local), rows_local), :
            ],
            send_sem=sum_send.at[source],
            recv_sem=sum_recv.at[source],
            device_id=(1 - layer, me),
            device_id_type=MESH,
        ).wait_recv()

    def task_sum(to):
        at = pl.ds(pl.multiple_of(to * width, width), width)
        result = held[0, :, at].astype(F32)
        for t in range(1, tasks):
            result = result + held[t, :, at].astype(F32)
        return result.astype(BF16)

    corners = ((y, c), (y, 1 - c), (1 - y, c), (1 - y, 1 - c))
    crossing = [
        row_of(zz, yy, cc)
        for yy, cc in corners
        for zz in (lax.rem(z + lines // 2, lines), lines - 1 - z)
    ]
    staying = [row_of(z + 1 - 2 * lax.rem(z, 2), yy, cc) for yy, cc in corners]
    staying += [row_of(z, yy, cc) for yy, cc in corners[1:]]
    queue = crossing + staying
    sum_copies = []

    def send_sums(count):
        for _ in range(min(count, len(queue))):
            to = queue.pop(0)
            sums[to] = task_sum(to)
            copy = sum_copy(to)
            copy.start()
            sum_copies.append(copy)

    for load in loads:
        load.wait()
    columns[pl.ds(pl.multiple_of(me * rows_local, rows_local), rows_local), :] = task_sum(me)
    use_basis(me)

    for tick in range(lines + 3):
        ready = []
        if 1 <= tick < lines:
            for zz, step, valid in at_distance(tick):
                block = row_of(zz, y, c)
                when(valid, functools.partial(got_basis, block, layer))
                onward = z + 1 < lines if step < 0 else z >= 1
                to_line(block, -step, jnp.logical_and(valid, onward))
                to_side(block, layer, valid)
                to_over(block, valid)
                to_core(block, layer, valid)
        if 0 <= tick - 1 < lines:
            for zz, _, valid in at_distance(tick - 1):
                block = row_of(zz, 1 - y, c)
                when(valid, functools.partial(got_basis, block, layer))
                to_core(block, layer, valid)
                if tick == 1:
                    got_basis(block, 1 - layer)
                    to_core(block, 1 - layer)
                    ready.append((block, None))
                else:
                    to_over(block, valid)
        if 1 <= tick - 2 < lines:
            for zz, _, valid in at_distance(tick - 2):
                for yy in (y, 1 - y):
                    block = row_of(zz, yy, c)
                    when(valid, functools.partial(got_basis, block, 1 - layer))
                    to_core(block, 1 - layer, valid)
                    ready.append((block, valid))
        if 0 <= tick - 3 < lines:
            for zz, _, valid in at_distance(tick - 3):
                for yy in (y, 1 - y):
                    block = row_of(zz, yy, 1 - c)
                    when(valid, functools.partial(got_basis, block, layer))
                    when(valid, functools.partial(got_basis, block, 1 - layer))
                    ready.append((block, valid))
        send_sums(PACE[tick])
        for block, valid in ready:
            when(valid, functools.partial(use_basis, block))

    def factor_place(block):
        return factors.at[pl.ds(pl.multiple_of(block * rows_local, rows_local), rows_local), :]

    def factor_copy(block, sem, to):
        return pltpu.make_async_remote_copy(
            src_ref=factor_place(block),
            dst_ref=factor_place(block),
            send_sem=sem,
            recv_sem=factor_recv.at[block],
            device_id=(layer, to),
            device_id_type=MESH,
        )

    def got_factor(block):
        factor_copy(block, factor_core.at[block], row_of(z, y, 1 - c)).wait_recv()

    own = [sketch[t].astype(BF16) for t in range(tasks)]
    factors[pl.ds(pl.multiple_of(me * rows_local, rows_local), rows_local), :] = jnp.concatenate(
        own, axis=1
    )
    for k in range(1, lines):
        to = row_of(lax.rem(z + k, lines), y, c)
        start(factor_copy(me, factor_line.at[k], to))

    def factor_to_side(block):
        start(factor_copy(block, factor_side.at[block], row_of(z, 1 - y, c)))

    def factor_to_core(block):
        start(factor_copy(block, factor_core.at[block], row_of(z, y, 1 - c)))

    factor_to_side(me)
    factor_to_core(me)
    send_sums(PACE[lines + 3])
    for k in range(1, lines):
        block = row_of(lax.rem(z + k, lines), y, c)
        got_factor(block)
        factor_to_side(block)
        factor_to_core(block)
    for k in range(lines):
        block = row_of(lax.rem(z + k, lines), 1 - y, c)
        got_factor(block)
        factor_to_core(block)
    for k in range(lines):
        for yy in (y, 1 - y):
            got_factor(row_of(lax.rem(z + k, lines), yy, 1 - c))

    send_sums(len(queue))

    size = aug.shape[0]
    aug[:, :size] = inner_rows(factors[...], factors[...])
    aug[:, size:] = jnp.where(
        lax.broadcasted_iota(jnp.int32, (size, size), 0)
        == lax.broadcasted_iota(jnp.int32, (size, size), 1),
        1.0,
        0.0,
    )
    chol_inverse(aug)
    rest = aug[:, size:]
    result = None
    for _ in range(3):
        piece = rest.astype(BF16)
        rest = rest - piece.astype(F32)
        term = outer_rows(factors[...], piece)
        result = term if result is None else result + term
    white[...] = result.astype(BF16)

    group = 4 * rows_local
    for k in range(lines):
        zz = lax.rem(z + k, lines)
        for yy, cc in ((y, c), (y, 1 - c), (1 - y, c), (1 - y, 1 - c)):
            if k == 0 and yy is y and cc is c:
                continue
            got_sum(row_of(zz, yy, cc))
        at = pl.ds(pl.multiple_of(zz * group, group), group)
        term = inner_rows(white[at, :], columns[at, :])
        if k == 0:
            total[...] = term
        elif k < lines - 1:
            total[...] += term
        else:
            coeffs[...] = (total[...] + term).astype(BF16)

    for copy, valid in sent:
        when(valid, copy.wait_send)

    for copy in sum_copies:
        copy.wait_send()


def line_shards(n, deltas, basis):
    tasks, rows_local, cols = deltas.shape[1:]
    depth, rank = basis.shape
    size = tasks * rank
    width = cols // n
    rows = rows_local * n
    lines = n // 4
    dma = pltpu.SemaphoreType.DMA
    white, coeffs = pl.pallas_call(
        functools.partial(kernel, lines),
        out_shape=(
            jax.ShapeDtypeStruct((rows, size), BF16),
            jax.ShapeDtypeStruct((size, width), BF16),
        ),
        in_specs=[pl.BlockSpec(memory_space=pl.ANY)] * 2,
        out_specs=[pl.BlockSpec(memory_space=pltpu.VMEM)] * 2,
        scratch_shapes=[
            pltpu.VMEM((tasks, rows_local, cols), BF16),
            pltpu.VMEM((n, rows_local, width), BF16),
            pltpu.VMEM((rows, width), BF16),
            pltpu.VMEM((n, depth, rank), BF16),
            pltpu.VMEM((rows, size), BF16),
            pltpu.VMEM((tasks, rows_local, rank), F32),
            pltpu.VMEM((size, 2 * size), F32),
            pltpu.VMEM((size, width), F32),
            dma((5,)),
            dma((n, 2)),
            dma((n, 2)),
            dma((n,)),
            dma((n, 2)),
            dma((n, 2)),
            dma((n,)),
            dma((n,)),
            dma((lines,)),
            dma((n,)),
            dma((n,)),
            dma((n,)),
        ],
        compiler_params=pltpu.CompilerParams(
            collective_id=0, has_side_effects=True, vmem_limit_bytes=60 * 2**20
        ),
        cost_estimate=pl.CostEstimate(
            flops=4 * rows * size * width, bytes_accessed=8 * 2**20, transcendentals=0
        ),
    )(deltas[0], basis)
    merged = lax.dot_general(
        white, coeffs, (((1,), (0,)), ((), ())), preferred_element_type=F32
    )
    return merged.astype(BF16)[None]


def solution(mesh):
    n = mesh.shape["row"]
    fits = n == 16 and mesh.shape["layer"] == 2
    return jax.shard_map(
        functools.partial(line_shards, n) if fits else general_shards,
        mesh=mesh,
        in_specs=(P("layer", None, "row", None), P("row", None)),
        out_specs=P("layer", None, "row"),
        check_vma=False,
    )
```

```python
import functools

import jax
import jax.numpy as jnp
from jax import lax
from jax.experimental import pallas as pl
from jax.experimental.pallas import tpu as pltpu
from jax.sharding import PartitionSpec as P

MESH = pl.DeviceIdType.MESH
F32 = jnp.float32
BF16 = jnp.bfloat16
EXACT = lax.Precision.HIGHEST
PANEL = 64
GROUP = 16
PACE = (0, 1, 1, 1, 0, 0, 0, 5)


def whiten_rows(factors, chol_factor):
    return lax.linalg.triangular_solve(
        chol_factor, factors.astype(jnp.float32), left_side=False, lower=True, transpose_a=True
    ).astype(jnp.bfloat16)


def inner_rows(left, right):
    return lax.dot_general(
        left, right, (((0,), (0,)), ((), ())), preferred_element_type=jnp.float32
    )


def outer_rows(left, right):
    return lax.dot_general(
        left, right, (((1,), (1,)), ((), ())), preferred_element_type=jnp.float32
    )


def general_shards(deltas, basis):
    group_deltas = deltas[0]
    task_count, rows_local, col_count = group_deltas.shape
    rank_width = basis.shape[1]
    factor_width = task_count * rank_width
    sketch = jnp.einsum(
        "trc,ck->trk",
        group_deltas,
        lax.all_gather(basis, "row", axis=0, tiled=True),
        preferred_element_type=jnp.float32,
    )
    factors = sketch.astype(jnp.bfloat16).transpose(1, 0, 2).reshape(rows_local, factor_width)
    gram_sum = lax.psum(inner_rows(factors, factors), "row")
    chol_factor = jnp.linalg.cholesky(gram_sum)
    local_white = whiten_rows(factors, chol_factor)
    whitened = lax.all_gather(local_white, "row", axis=0, tiled=True)
    task_sum = jnp.sum(group_deltas.astype(jnp.float32), axis=0).astype(jnp.bfloat16)
    columns = lax.all_to_all(task_sum, "row", split_axis=1, concat_axis=0, tiled=True)
    coeffs = inner_rows(columns, whitened).astype(jnp.bfloat16)
    merged = lax.dot_general(
        whitened, coeffs, (((1,), (1,)), ((), ())), preferred_element_type=jnp.float32
    )
    return merged.astype(jnp.bfloat16)[None]


def panel_inverse(block):
    shape = block.shape
    row = lax.broadcasted_iota(jnp.int32, shape, 0)
    lane = lax.broadcasted_iota(jnp.int32, shape, 1)
    work = jnp.where(lane < PANEL, block, 0.0) + jnp.where(lane == row + PANEL, 1.0, 0.0)
    pivots = jnp.ones(shape, F32)
    for start in range(0, PANEL, GROUP):
        cols = [
            jnp.broadcast_to(work[:, j : j + 1], shape) for j in range(start, start + GROUP)
        ]
        for at in range(GROUP):
            j = start + at
            pivot = cols[at][j : j + 1, :]
            pivots = jnp.where(row == j, pivot, pivots)
            scale = jnp.where(row > j, cols[at] * (1.0 / pivot), 0.0)
            work = work - scale * work[j : j + 1, :]
            for later in range(at + 1, GROUP):
                cols[later] = cols[later] - scale * cols[later][j : j + 1, :]
    root = lax.rsqrt(pivots)
    root = root * (1.5 - 0.5 * pivots * root * root)
    return (work * root)[:, PANEL : 2 * PANEL]


def chol_inverse(aug):
    size = aug.shape[0]
    for at in range(0, size, PANEL):
        after = at + PANEL
        rows = aug[at:after, :]
        inverse = panel_inverse(rows[:, at : at + 128] if at % 128 == 0 else pltpu.roll(
            rows[:, at - at % 128 : at - at % 128 + 128], 128 - at % 128, 1
        ))
        done = lax.dot_general(
            inverse, rows, (((1,), (0,)), ((), ())), precision=EXACT, preferred_element_type=F32
        )
        if after < size:
            aug[after:, :] -= lax.dot_general(
                done[:, after:size],
                done,
                (((0,), (0,)), ((), ())),
                precision=EXACT,
                preferred_element_type=F32,
            )
        aug[at:after, :] = done


def kernel(
    lines,
    deltas,
    basis,
    white,
    coeffs,
    held,
    sums,
    columns,
    bases,
    factors,
    sketch,
    aug,
    total,
    load_sem,
    basis_line,
    basis_side,
    basis_over,
    basis_core,
    basis_recv,
    sum_send,
    sum_recv,
    factor_line,
    factor_side,
    factor_core,
    factor_recv,
):
    layer = lax.axis_index("layer")
    me = lax.axis_index("row")
    z, y, c = me // 4, lax.rem(me // 2, 2), lax.rem(me, 2)
    n = 4 * lines
    depth = basis.shape[0]
    half = depth // 2
    tasks, rows_local, _ = held.shape
    width = columns.shape[1]

    def row_of(zz, yy, cc):
        return (zz * 2 + yy) * 2 + cc

    chunk = held.shape[2] // 4
    loads = []
    for i in range(4):
        load = pltpu.make_async_copy(
            deltas.at[:, :, pl.ds(i * chunk, chunk)],
            held.at[:, :, pl.ds(i * chunk, chunk)],
            load_sem.at[i],
        )
        load.start()
        loads.append(load)

    own_basis = pltpu.make_async_copy(basis, bases.at[me], load_sem.at[4])
    own_basis.start()

    barrier = pltpu.get_barrier_semaphore()
    for k in range(1, n):
        pl.semaphore_signal(
            barrier, inc=1, device_id=(layer, lax.rem(me + k, n)), device_id_type=MESH
        )
    pl.semaphore_signal(barrier, inc=1, device_id=(1 - layer, me), device_id_type=MESH)
    sketch[...] = jnp.zeros_like(sketch)
    own_basis.wait()
    pl.semaphore_wait(barrier, n)

    sent = []

    def start(copy, valid=None):
        if valid is None:
            copy.start()
        else:
            pl.when(valid)(copy.start)
        sent.append((copy, valid))

    def basis_copy(block, part, sem, to):
        place = bases.at[block, pl.ds(pl.multiple_of(part * half, half), half), :]
        return pltpu.make_async_remote_copy(
            src_ref=place,
            dst_ref=place,
            send_sem=sem,
            recv_sem=basis_recv.at[block, part],
            device_id=to,
            device_id_type=MESH,
        )

    def got_basis(block, part):
        basis_copy(block, part, basis_core.at[block, part], (1 - layer, me)).wait_recv()

    def to_side(block, part, valid=None):
        start(
            basis_copy(
                block, part, basis_side.at[block, part], (layer, row_of(z, 1 - y, c))
            ),
            valid,
        )

    def to_over(block, valid=None):
        start(basis_copy(block, layer, basis_over.at[block], (1 - layer, me)), valid)

    def to_core(block, part, valid=None):
        start(
            basis_copy(
                block, part, basis_core.at[block, part], (layer, row_of(z, y, 1 - c))
            ),
            valid,
        )

    def to_line(block, step, valid):
        start(
            basis_copy(block, layer, basis_line.at[block, (step + 1) // 2], (layer, row_of(z + step, y, c))),
            valid,
        )

    def use_basis(block):
        at = pl.multiple_of(block * depth, depth)
        left = held[:, :, pl.ds(at, depth)].reshape(tasks * rows_local, depth)
        sketch[...] += jnp.dot(left, bases[block], preferred_element_type=F32).reshape(sketch.shape)

    def when(valid, run):
        if valid is None:
            run()
        else:
            pl.when(valid)(run)

    def at_distance(d):
        if d == 0:
            return [(z, 0, None)]
        return [(z - d, -1, z - d >= 0), (z + d, 1, z + d < lines)]

    to_line(me, 1, z + 1 < lines)
    to_line(me, -1, z >= 1)
    to_side(me, layer)
    to_side(me, 1 - layer)
    to_core(me, layer)
    to_core(me, 1 - layer)

    def sum_copy(to):
        return pltpu.make_async_remote_copy(
            src_ref=sums.at[to],
            dst_ref=columns.at[pl.ds(pl.multiple_of(me * rows_local, rows_local), rows_local), :],
            send_sem=sum_send.at[to],
            recv_sem=sum_recv.at[me],
            device_id=(layer, to),
            device_id_type=MESH,
        )

    def got_sum(source):
        pltpu.make_async_remote_copy(
            src_ref=sums.at[source],
            dst_ref=columns.at[
                pl.ds(pl.multiple_of(source * rows_local, rows_local), rows_local), :
            ],
            send_sem=sum_send.at[source],
            recv_sem=sum_recv.at[source],
            device_id=(1 - layer, me),
            device_id_type=MESH,
        ).wait_recv()

    def task_sum(to):
        at = pl.ds(pl.multiple_of(to * width, width), width)
        result = held[0, :, at].astype(F32)
        for t in range(1, tasks):
            result = result + held[t, :, at].astype(F32)
        return result.astype(BF16)

    corners = ((y, c), (y, 1 - c), (1 - y, c), (1 - y, 1 - c))
    crossing = [
        row_of(zz, yy, cc)
        for yy, cc in corners
        for zz in (lax.rem(z + lines // 2, lines), lines - 1 - z)
    ]
    staying = [row_of(z + 1 - 2 * lax.rem(z, 2), yy, cc) for yy, cc in corners]
    staying += [row_of(z, yy, cc) for yy, cc in corners[1:]]
    queue = crossing + staying
    sum_copies = []

    def send_sums(count):
        for _ in range(min(count, len(queue))):
            to = queue.pop(0)
            sums[to] = task_sum(to)
            copy = sum_copy(to)
            copy.start()
            sum_copies.append(copy)

    for load in loads:
        load.wait()
    columns[pl.ds(pl.multiple_of(me * rows_local, rows_local), rows_local), :] = task_sum(me)
    use_basis(me)

    for tick in range(lines + 3):
        ready = []
        if 1 <= tick < lines:
            for zz, step, valid in at_distance(tick):
                block = row_of(zz, y, c)
                when(valid, functools.partial(got_basis, block, layer))
                onward = z + 1 < lines if step < 0 else z >= 1
                to_line(block, -step, jnp.logical_and(valid, onward))
                to_side(block, layer, valid)
                to_over(block, valid)
                to_core(block, layer, valid)
        if 0 <= tick - 1 < lines:
            for zz, _, valid in at_distance(tick - 1):
                block = row_of(zz, 1 - y, c)
                when(valid, functools.partial(got_basis, block, layer))
                to_core(block, layer, valid)
                if tick == 1:
                    got_basis(block, 1 - layer)
                    to_core(block, 1 - layer)
                    ready.append((block, None))
                else:
                    to_over(block, valid)
        if 1 <= tick - 2 < lines:
            for zz, _, valid in at_distance(tick - 2):
                for yy in (y, 1 - y):
                    block = row_of(zz, yy, c)
                    when(valid, functools.partial(got_basis, block, 1 - layer))
                    to_core(block, 1 - layer, valid)
                    ready.append((block, valid))
        if 0 <= tick - 3 < lines:
            for zz, _, valid in at_distance(tick - 3):
                for yy in (y, 1 - y):
                    block = row_of(zz, yy, 1 - c)
                    when(valid, functools.partial(got_basis, block, layer))
                    when(valid, functools.partial(got_basis, block, 1 - layer))
                    ready.append((block, valid))
        send_sums(PACE[tick])
        for block, valid in ready:
            when(valid, functools.partial(use_basis, block))

    def factor_place(block):
        return factors.at[pl.ds(pl.multiple_of(block * rows_local, rows_local), rows_local), :]

    def factor_copy(block, sem, to):
        return pltpu.make_async_remote_copy(
            src_ref=factor_place(block),
            dst_ref=factor_place(block),
            send_sem=sem,
            recv_sem=factor_recv.at[block],
            device_id=(layer, to),
            device_id_type=MESH,
        )

    def got_factor(block):
        factor_copy(block, factor_core.at[block], row_of(z, y, 1 - c)).wait_recv()

    own = [sketch[t].astype(BF16) for t in range(tasks)]
    factors[pl.ds(pl.multiple_of(me * rows_local, rows_local), rows_local), :] = jnp.concatenate(
        own, axis=1
    )
    for k in range(1, lines):
        to = row_of(lax.rem(z + k, lines), y, c)
        start(factor_copy(me, factor_line.at[k], to))

    def factor_to_side(block):
        start(factor_copy(block, factor_side.at[block], row_of(z, 1 - y, c)))

    def factor_to_core(block):
        start(factor_copy(block, factor_core.at[block], row_of(z, y, 1 - c)))

    factor_to_side(me)
    factor_to_core(me)
    send_sums(PACE[lines + 3])
    for k in range(1, lines):
        block = row_of(lax.rem(z + k, lines), y, c)
        got_factor(block)
        factor_to_side(block)
        factor_to_core(block)
    for k in range(lines):
        block = row_of(lax.rem(z + k, lines), 1 - y, c)
        got_factor(block)
        factor_to_core(block)
    for k in range(lines):
        for yy in (y, 1 - y):
            got_factor(row_of(lax.rem(z + k, lines), yy, 1 - c))

    send_sums(len(queue))

    size = aug.shape[0]
    aug[:, :size] = inner_rows(factors[...], factors[...])
    aug[:, size:] = jnp.where(
        lax.broadcasted_iota(jnp.int32, (size, size), 0)
        == lax.broadcasted_iota(jnp.int32, (size, size), 1),
        1.0,
        0.0,
    )
    chol_inverse(aug)
    rest = aug[:, size:]
    result = None
    for _ in range(3):
        piece = rest.astype(BF16)
        rest = rest - piece.astype(F32)
        term = outer_rows(factors[...], piece)
        result = term if result is None else result + term
    white[...] = result.astype(BF16)

    group = 4 * rows_local
    for k in range(lines):
        zz = lax.rem(z + k, lines)
        for yy, cc in ((y, c), (y, 1 - c), (1 - y, c), (1 - y, 1 - c)):
            if k == 0 and yy is y and cc is c:
                continue
            got_sum(row_of(zz, yy, cc))
        at = pl.ds(pl.multiple_of(zz * group, group), group)
        term = inner_rows(white[at, :], columns[at, :])
        if k == 0:
            total[...] = term
        elif k < lines - 1:
            total[...] += term
        else:
            coeffs[...] = (total[...] + term).astype(BF16)

    for copy, valid in sent:
        when(valid, copy.wait_send)

    for copy in sum_copies:
        copy.wait_send()


def line_shards(n, deltas, basis):
    tasks, rows_local, cols = deltas.shape[1:]
    depth, rank = basis.shape
    size = tasks * rank
    width = cols // n
    rows = rows_local * n
    lines = n // 4
    dma = pltpu.SemaphoreType.DMA
    white, coeffs = pl.pallas_call(
        functools.partial(kernel, lines),
        out_shape=(
            jax.ShapeDtypeStruct((rows, size), BF16),
            jax.ShapeDtypeStruct((size, width), BF16),
        ),
        in_specs=[pl.BlockSpec(memory_space=pl.ANY)] * 2,
        out_specs=[pl.BlockSpec(memory_space=pltpu.VMEM)] * 2,
        scratch_shapes=[
            pltpu.VMEM((tasks, rows_local, cols), BF16),
            pltpu.VMEM((n, rows_local, width), BF16),
            pltpu.VMEM((rows, width), BF16),
            pltpu.VMEM((n, depth, rank), BF16),
            pltpu.VMEM((rows, size), BF16),
            pltpu.VMEM((tasks, rows_local, rank), F32),
            pltpu.VMEM((size, 2 * size), F32),
            pltpu.VMEM((size, width), F32),
            dma((5,)),
            dma((n, 2)),
            dma((n, 2)),
            dma((n,)),
            dma((n, 2)),
            dma((n, 2)),
            dma((n,)),
            dma((n,)),
            dma((lines,)),
            dma((n,)),
            dma((n,)),
            dma((n,)),
        ],
        compiler_params=pltpu.CompilerParams(
            collective_id=0, has_side_effects=True, vmem_limit_bytes=60 * 2**20
        ),
        cost_estimate=pl.CostEstimate(
            flops=4 * rows * size * width, bytes_accessed=8 * 2**20, transcendentals=0
        ),
    )(deltas[0], basis)
    merged = lax.dot_general(
        white, coeffs, (((1,), (0,)), ((), ())), preferred_element_type=F32
    )
    return merged.astype(BF16)[None]


def solution(mesh):
    n = mesh.shape["row"]
    fits = n == 16 and mesh.shape["layer"] == 2
    return jax.shard_map(
        functools.partial(line_shards, n) if fits else general_shards,
        mesh=mesh,
        in_specs=(P("layer", None, "row", None), P("row", None)),
        out_specs=P("layer", None, "row"),
        check_vma=False,
    )
```
